32 devices in a mesh: req: 16 (over z, y, x), head: 2 (over core).
Axes of the slice: x: 2, y: 2, z: 4, core: 2. Of those that a mesh axis runs over, the one named last changes fastest.
Arguments:
- inner_input: bfloat16 [4096, 16384], P('req', 'head'), may hold values from -6 to 6
- projection_input: bfloat16 [4096, 8, 2, 128], P('req', 'head'), may hold values from -6 to 6
- step_before_bias: bfloat16 [4096, 256], P('req', 'head'), may hold values from -2 to 11
- inner_conv_taps: float32 [4, 16384], P(None, 'head'), may hold values from -3 to 3
- projection_conv_taps: float32 [4, 8, 2, 128], P(None, 'head'), may hold values from -3 to 3
- step_bias: float32 [256], P('head'), may hold values from -4.5 to -3.5
- head_decay_rate: float32 [256], P('head'), may hold values from 0.1 to 3
- head_skip_gain: float32 [256], P('head'), may hold values from 0.5 to 1.5
- group_norm_gain: float32 [16384], P('head'), may hold values from 0.5 to 1.5
- tenant: int32 [16], P('req'), may hold values from 0 to 15
- tenant_adapter_row: int32 [16], replicated, may hold values from 0 to 15, each once
- cache_holder_index: int32 [16], P('req'), may hold values from 0 to 15, as said below
- cache_slot_index: int32 [16], P('req'), may hold values from 0 to 1
- adapter_down_panels: bfloat16 [16, 16384, 64], P('req', 'head'), may hold values from -0.046875 to 0.046875
- adapter_up_panels: bfloat16 [16, 64, 8192], P('req', None, 'head'), may hold values from -0.75 to 0.75
- cached_ssm_states: bfloat16 [32, 256, 64, 128], P('req', 'head'), may hold values from -2.5 to 2.5
- inner_conv_cache: bfloat16 [32, 3, 16384], P('req', None, 'head'), may hold values from -6 to 6
- projection_conv_cache: bfloat16 [32, 3, 8, 2, 128], P('req', None, 'head'), may hold values from -6 to 6
Outputs:
- normed_output: bfloat16 [4096, 16384], P('req', 'head')
- adapter_output_term: bfloat16 [4096, 8192], P('req', 'head')
- updated_state: bfloat16 [16, 256, 64, 128], P('req', 'head')
The draws below stay inside these ranges and needn't reach their ends.
Inputs may be any that keep to these rules, and one draw needn't show every extreme that they name: `tenant_adapter_row`: every row of the adapter tables belongs to exactly one tenant. `cache_holder_index`: no two requests share a cache slot, and each index of req holds the cached states of exactly 1 request.
All inputs are finite; a program needn't handle non-finite values.
Results may differ from the reference program's by a relative error of at most 0.013.
Values may be sent and summed in bfloat16 or wider, within the bound.
A program may use at most 128 MiB of HBM per device.

```python
import math
import jax
import jax.numpy as jnp
import numpy as np
from jax import lax

MODEL_WIDTH = 8192
HEADS = 256
P_SIZE = 64
N = 128
G = 8
K = 4
ADAPTER_RANK = 64
FRESH_ITEMS = 256
REQ_DEV = 1
INNER_CHANNELS = 16384
REQUESTS = 16
SUMMED_ITEMS = 4096
SLOTS_DEV = 2
SLOTS = 32
TENANT_COUNT = 16


def memo_location(key):
    base_key = jax.random.fold_in(key, 11)
    placing = jax.random.permutation(jax.random.fold_in(base_key, 1), REQUESTS)
    spread_factor = SLOTS_DEV // REQ_DEV
    side = jax.random.randint(jax.random.fold_in(base_key, 2), (REQUESTS,), 0, spread_factor)
    owner = (placing // REQ_DEV).astype(jnp.int32)
    slot = (placing % REQ_DEV * spread_factor + side).astype(jnp.int32)
    return (owner, slot)


def draw_cache_holder_index(key, part):
    return memo_location(key)[0]


def draw_cache_slot_index(key, part):
    return memo_location(key)[1]


def draw_step_before_bias(key, part):
    noise_key = jax.random.fold_in(key, 3)
    spike_seed_handle = jax.random.fold_in(key, 4)
    growth_prng_stream = jax.random.fold_in(key, 5)
    baseline_noise_part = jnp.clip(0.5 * jax.random.normal(noise_key, (SUMMED_ITEMS, HEADS), jnp.float32), -2.0, 2.0)
    spike_magnitudes = jax.random.randint(spike_seed_handle, (SUMMED_ITEMS, 1), 0, max(FRESH_ITEMS // 3, 2)) == 0
    raise_offset = jax.random.uniform(growth_prng_stream, (SUMMED_ITEMS, 1), jnp.float32, 7.0, 9.0)
    return jnp.where(spike_magnitudes, baseline_noise_part + raise_offset, baseline_noise_part).astype(jnp.bfloat16)


def draw_head_decay_rate(key, part):
    rate_key = jax.random.fold_in(key, 6)
    upper = 3.0
    dispersion_factor = jax.random.uniform(rate_key, (HEADS,), jnp.float32, math.log(0.1), math.log(upper))
    return jnp.exp(dispersion_factor).astype(jnp.float32)


def touch_ends(result, rng, low, largest):
    shape = result.shape
    place = [jax.random.randint(jax.random.fold_in(rng, axis), (), 0, shape[axis]) for axis in range(len(shape))]
    result = result.at[tuple(place)].set(low)
    longest = shape.index(max(shape))
    place[longest] = (place[longest] + 1) % shape[longest]
    return result.at[tuple(place)].set(largest)


def steps_of(key, extent, shards, smallest, top_value):
    loudness = 1.0
    for position, parts in shards:
        steps = jax.random.uniform(jax.random.fold_in(jax.random.fold_in(key, 6), position), (parts,), jnp.float32, smallest / len(shards), top_value / len(shards))
        loudness = loudness * jnp.repeat(jnp.exp(steps), extent[position] // parts).reshape((-1,) + (1,) * (len(extent) - 1 - position))
    return loudness


def rank_bounds(number_of, slope):
    weights = [(1 << 20) // math.isqrt(standing ** slope) + 1 for standing in range(1, number_of + 1)]
    width = 1 + sum(weights) // (1 << 30)
    return np.cumsum(np.array([max(1, weight // width) for weight in weights]))


def ranked(stream_key, extent, count, lean):
    table = rank_bounds(count, lean)
    pick = jax.random.randint(jax.random.fold_in(stream_key, 1), extent, 0, int(table[count - 1]))
    standing = jnp.searchsorted(jnp.asarray(table, jnp.int32), pick, side="right")
    return jax.random.permutation(jax.random.fold_in(stream_key, 2), count)[standing].astype(jnp.int32)


def centred(rng, extent, width, bound, pieces=(), kind=jnp.bfloat16):
    values = jax.random.normal(rng, extent, jnp.float32) * width
    if len(pieces) > 0:
        values = steps_of(rng, extent, pieces, -0.22, 0.18) * values
    return jnp.clip(values, min=-bound, max=bound).astype(kind)


def setup_inputs(seed: int = 0) -> dict:
    seeds = jax.random.split(jax.random.key(seed), 19)
    inner_input = centred(seeds[0], (SUMMED_ITEMS, INNER_CHANNELS), 1.0, 6.0, ((0, 16), (1, 2)))
    projection_input = centred(seeds[1], (SUMMED_ITEMS, G, 2, N), 1.0, 6.0, ((0, 16), (1, 2)))
    step_before_bias = draw_step_before_bias(jax.random.fold_in(seeds[18], 71), 0)
    inner_conv_taps = centred(seeds[3], (K, INNER_CHANNELS), K ** -0.5, 3.0, ((1, 2),), jnp.float32)
    projection_conv_taps = centred(seeds[4], (K, G, 2, N), K ** -0.5, 3.0, ((1, 2),), jnp.float32)
    step_bias = jnp.clip(-4.5 + 1.0 * jax.random.uniform(seeds[5], (HEADS,), jnp.float32) ** steps_of(seeds[5], (HEADS,), ((0, 2),), -0.2, 0.2), -4.5, -3.5)
    head_decay_rate = draw_head_decay_rate(jax.random.fold_in(seeds[18], 71), 0)
    head_skip_gain = jnp.clip(0.5 + 1.0 * jax.random.uniform(seeds[7], (HEADS,), jnp.float32) ** steps_of(seeds[7], (HEADS,), ((0, 2),), -0.2, 0.2), 0.5, 1.5)
    group_norm_gain = jnp.clip(1.0 + 0.1 * jax.random.normal(seeds[8], (INNER_CHANNELS,), jnp.float32), 0.5, 1.5)
    tenant = touch_ends(ranked(seeds[9], (REQUESTS,), TENANT_COUNT, 2), jax.random.fold_in(seeds[9], 3), 0, TENANT_COUNT - 1).astype(jnp.int32)
    tenant_adapter_row = jax.random.permutation(seeds[10], TENANT_COUNT).astype(jnp.int32)
    cache_holder_index = draw_cache_holder_index(jax.random.fold_in(seeds[18], 71), 0)
    cache_slot_index = draw_cache_slot_index(jax.random.fold_in(seeds[18], 71), 0)
    adapter_down_panels = centred(seeds[13], (TENANT_COUNT, INNER_CHANNELS, ADAPTER_RANK), INNER_CHANNELS ** -0.5, 0.046875, ((0, 16), (1, 2)))
    adapter_up_panels = centred(seeds[14], (TENANT_COUNT, ADAPTER_RANK, MODEL_WIDTH), ADAPTER_RANK ** -0.5, 0.75, ((0, 16), (2, 2)))
    cached_ssm_states = centred(seeds[15], (SLOTS, HEADS, P_SIZE, N), 0.3, 2.5, ((0, 16), (1, 2)))
    inner_conv_cache = centred(seeds[16], (SLOTS, K - 1, INNER_CHANNELS), 1.0, 6.0, ((0, 16), (2, 2)))
    projection_conv_cache = centred(seeds[17], (SLOTS, K - 1, G, 2, N), 1.0, 6.0, ((0, 16), (2, 2)))
    return {"inner_input": inner_input, "projection_input": projection_input, "step_before_bias": step_before_bias, "inner_conv_taps": inner_conv_taps, "projection_conv_taps": projection_conv_taps, "step_bias": step_bias, "head_decay_rate": head_decay_rate, "head_skip_gain": head_skip_gain, "group_norm_gain": group_norm_gain, "tenant": tenant, "tenant_adapter_row": tenant_adapter_row, "cache_holder_index": cache_holder_index, "cache_slot_index": cache_slot_index, "adapter_down_panels": adapter_down_panels, "adapter_up_panels": adapter_up_panels, "cached_ssm_states": cached_ssm_states, "inner_conv_cache": inner_conv_cache, "projection_conv_cache": projection_conv_cache}


ADAPTER_SCALE = 2.0
NORM_EPSILON = 1e-05

def causal_conv(cached, current, weight):
    joined = jnp.concatenate([cached, current], axis=0).astype(jnp.float32)
    length_value = current.shape[0]
    summed = weight[0] * joined[0:length_value]
    for tap in range(1, weight.shape[0]):
        summed = summed + weight[tap] * joined[tap:tap + length_value]
    return jax.nn.silu(summed).astype(jnp.bfloat16)

def reference(inner_input, projection_input, step_before_bias, inner_conv_taps, projection_conv_taps, step_bias, head_decay_rate, head_skip_gain, group_norm_gain, tenant, tenant_adapter_row, cache_holder_index, cache_slot_index, adapter_down_panels, adapter_up_panels, cached_ssm_states, inner_conv_cache, projection_conv_cache):
    cache_rows = (cache_holder_index * SLOTS_DEV + cache_slot_index).astype(jnp.int32)
    adapter_rows = jnp.take(tenant_adapter_row, tenant).astype(jnp.int32)
    x_blocks = inner_input.reshape(REQUESTS, FRESH_ITEMS, INNER_CHANNELS)
    bc_blocks = projection_input.reshape(REQUESTS, FRESH_ITEMS, G, 2, N)
    unprocessed_sequence_blocks = step_before_bias.reshape(REQUESTS, FRESH_ITEMS, HEADS)
    per_group = HEADS // G
    positions = jnp.arange(FRESH_ITEMS, dtype=jnp.int32)
    causal = positions[:, None] >= positions[None, :]

    def one_request(request_items):
        x_req, bc_req, raw_req, cache_row, adapter_position = request_items
        cached_state = lax.dynamic_index_in_dim(cached_ssm_states, cache_row, 0, keepdims=False)
        cached_x = lax.dynamic_index_in_dim(inner_conv_cache, cache_row, 0, keepdims=False)
        cached_bc = lax.dynamic_index_in_dim(projection_conv_cache, cache_row, 0, keepdims=False)
        down_panel = lax.dynamic_index_in_dim(adapter_down_panels, adapter_position, 0, keepdims=False)
        up_panel = lax.dynamic_index_in_dim(adapter_up_panels, adapter_position, 0, keepdims=False)
        conv_x = causal_conv(cached_x, x_req, inner_conv_taps)
        conv_bc = causal_conv(cached_bc, bc_req, projection_conv_taps)
        b_proj = conv_bc[:, :, 0, :].astype(jnp.float32)
        c_proj = conv_bc[:, :, 1, :].astype(jnp.float32)
        step_size = jax.nn.softplus(raw_req.astype(jnp.float32) + step_bias)
        log_decay = jnp.cumsum(-head_decay_rate * step_size, axis=0)
        score_bc = jnp.einsum('tgn,sgn->gts', c_proj, b_proj)
        score_heads = jnp.repeat(score_bc, per_group, axis=0)
        log_gap = log_decay.T[:, :, None] - log_decay.T[:, None, :]
        decay_factor = jnp.exp(jnp.where(causal[None], log_gap, -jnp.inf))
        mix_weights = (score_heads * decay_factor * step_size.T[:, None, :]).astype(jnp.bfloat16)
        conv_heads = conv_x.reshape(FRESH_ITEMS, HEADS, P_SIZE).astype(jnp.float32)
        intra = jnp.einsum('hts,shp->thp', mix_weights.astype(jnp.float32), conv_heads)
        c_heads = jnp.repeat(c_proj, per_group, axis=1)
        inter = jnp.einsum('thn,hpn->thp', c_heads, cached_state.astype(jnp.float32)) * jnp.exp(log_decay)[:, :, None]
        mixed = intra + inter + head_skip_gain[None, :, None] * conv_heads
        grouped = mixed.reshape(FRESH_ITEMS, G, per_group * P_SIZE)
        mean_square = lax.optimization_barrier(jnp.mean(grouped * grouped, axis=2, keepdims=True))
        normed_output = ((grouped * lax.rsqrt(mean_square + NORM_EPSILON)).reshape(FRESH_ITEMS, INNER_CHANNELS) * group_norm_gain).astype(jnp.bfloat16)
        reduced_rank = jnp.dot(normed_output, down_panel, preferred_element_type=jnp.float32).astype(jnp.bfloat16)
        adapter_output_term = (jnp.dot(reduced_rank, up_panel, preferred_element_type=jnp.float32) * ADAPTER_SCALE).astype(jnp.bfloat16)
        log_total = log_decay[-1]
        carry_weight = jnp.exp(log_total[None, :] - log_decay) * step_size
        carried = (conv_heads * carry_weight[:, :, None]).astype(jnp.bfloat16)
        b_heads = jnp.repeat(b_proj, per_group, axis=1)
        fresh_state = jnp.einsum('shp,shn->hpn', carried.astype(jnp.float32), b_heads)
        updated_state = fresh_state + jnp.exp(log_total)[:, None, None] * cached_state.astype(jnp.float32)
        return (normed_output, adapter_output_term, updated_state.astype(jnp.bfloat16))
    result_list = lax.map(one_request, (x_blocks, bc_blocks, unprocessed_sequence_blocks, cache_rows, adapter_rows))
    output_gathered, adapter_term_all, state_gathered = result_list
    return (output_gathered.reshape(SUMMED_ITEMS, INNER_CHANNELS), adapter_term_all.reshape(SUMMED_ITEMS, MODEL_WIDTH), state_gathered)
```

```python
import jax
import jax.numpy as jnp
from jax import lax
from jax.sharding import PartitionSpec as P

ADAPTER_SCALE = 2.0
NORM_EPSILON = 1e-05


def causal_conv(cached, current, weight):
    joined = jnp.concatenate([cached, current], axis=1)
    length_value = current.shape[1]
    summed = weight[0] * joined[:, 0:length_value]
    for tap in range(1, weight.shape[0]):
        summed = summed + weight[tap] * joined[:, tap : tap + length_value]
    return jax.nn.silu(summed).astype(jnp.bfloat16)


def per_device(
    inner_input,
    projection_input,
    step_before_bias,
    inner_conv_taps,
    projection_conv_taps,
    step_bias,
    head_decay_rate,
    head_skip_gain,
    group_norm_gain,
    tenant,
    tenant_adapter_row,
    cache_holder_index,
    cache_slot_index,
    adapter_down_panels,
    adapter_up_panels,
    cached_ssm_states,
    inner_conv_cache,
    projection_conv_cache,
):
    per_device_share = tenant.shape[0]
    slots_dev = cached_ssm_states.shape[0]
    hidden_features_on_card = inner_input.shape[1]
    heads_dev = step_before_bias.shape[1]
    groups_dev = projection_input.shape[1]
    state_size = projection_input.shape[3]
    head_size = hidden_features_on_card // heads_dev
    per_group = heads_dev // groups_dev
    reduced_width = adapter_down_panels.shape[2]
    model_per_device = adapter_up_panels.shape[2]
    tap_count = inner_conv_taps.shape[0]
    length_value = inner_input.shape[0] // per_device_share
    n = lax.axis_size("req")
    me = lax.axis_index("req")
    rows = slots_dev * (tap_count - 1)
    numbers = jnp.stack([tenant, cache_holder_index, cache_slot_index], axis=1)
    numbers = numbers.reshape(1, -1).astype(jnp.bfloat16)
    numbers = jnp.pad(numbers, ((0, rows - 1), (0, 128 - numbers.shape[1])))
    small = jnp.concatenate(
        [
            inner_conv_cache.reshape(rows, hidden_features_on_card),
            projection_conv_cache.reshape(rows, groups_dev * 2 * state_size),
            numbers,
        ],
        axis=1,
    )
    panels = jnp.concatenate(
        [
            jnp.transpose(adapter_down_panels[0].reshape(n, -1, reduced_width), (0, 2, 1)),
            jnp.transpose(adapter_up_panels[0].reshape(reduced_width, n, -1), (1, 0, 2)),
        ],
        axis=2,
    )
    down_piece = hidden_features_on_card // n
    panels = lax.all_to_all(panels, "req", split_axis=0, concat_axis=0, tiled=True)
    small_all = lax.all_gather(small, "req", axis=0, tiled=False)
    index_base = small.shape[1] - 128
    meta = small_all[:, 0, index_base : index_base + 3].astype(jnp.int32)
    tenant_all, owner_all, slot_all = meta[:, 0], meta[:, 1], meta[:, 2]
    picked_row = jnp.take(tenant_adapter_row, tenant_all, axis=0, mode="clip")
    my_slot = jnp.sum(jnp.where(owner_all == me, slot_all, 0))
    my_state = lax.dynamic_index_in_dim(cached_ssm_states, my_slot, 0, keepdims=False)
    state_pieces = my_state.reshape(n, heads_dev * head_size // n, state_size)
    state_pieces = lax.all_to_all(state_pieces, "req", split_axis=0, concat_axis=0, tiled=True)
    state_pieces = jnp.take(state_pieces, owner_all, axis=0, mode="clip")
    state_pieces = lax.all_to_all(state_pieces, "req", split_axis=0, concat_axis=0, tiled=True)
    panels = jnp.take(panels, picked_row, axis=0, mode="clip")
    panels, state_pieces = lax.optimization_barrier((panels, state_pieces))
    panels = lax.all_to_all(panels, "req", split_axis=0, concat_axis=0, tiled=True)
    down_t = jnp.transpose(panels[:, :, :down_piece], (1, 0, 2)).reshape(
        reduced_width, hidden_features_on_card
    )
    up_panel = jnp.transpose(panels[:, :, down_piece:], (1, 0, 2)).reshape(
        per_device_share, reduced_width, model_per_device
    )
    cached_state = state_pieces.reshape(
        per_device_share, groups_dev, per_group, head_size, state_size
    )
    mine = lax.dynamic_slice(
        small_all,
        (cache_holder_index[0], cache_slot_index[0] * (tap_count - 1), 0),
        (1, tap_count - 1, small.shape[1]),
    )
    cached_x = mine[:, :, :hidden_features_on_card]
    cached_bc = mine[:, :, hidden_features_on_card:index_base].reshape(
        1, tap_count - 1, groups_dev, 2, state_size
    )
    conv_x = causal_conv(
        cached_x,
        inner_input.reshape(per_device_share, length_value, hidden_features_on_card),
        inner_conv_taps,
    )
    conv_bc = causal_conv(
        cached_bc,
        projection_input.reshape(per_device_share, length_value, groups_dev, 2, state_size),
        projection_conv_taps,
    )
    b_proj = conv_bc[:, :, :, 0]
    c_proj = conv_bc[:, :, :, 1]
    step_size = jax.nn.softplus(step_before_bias.astype(jnp.float32) + step_bias).reshape(
        per_device_share, length_value, heads_dev
    )
    log_decay = jnp.cumsum(-head_decay_rate * step_size, axis=1)
    log_decay5 = log_decay.reshape(per_device_share, length_value, groups_dev, per_group)
    step_size5 = step_size.reshape(per_device_share, length_value, groups_dev, per_group)
    score_bc = jnp.einsum("rtgn,rsgn->rgts", c_proj, b_proj, preferred_element_type=jnp.float32)
    decay_rows = jnp.transpose(log_decay5, (0, 2, 3, 1))
    log_gap = decay_rows[..., :, None] - decay_rows[..., None, :]
    token_ids = jnp.arange(length_value, dtype=jnp.int32)
    causal = token_ids[:, None] >= token_ids[None, :]
    decay_factor = jnp.exp(jnp.where(causal, log_gap, -jnp.inf))
    step_rows = jnp.transpose(step_size5, (0, 2, 3, 1))
    mix_weights = (score_bc[:, :, None] * decay_factor * step_rows[..., None, :]).astype(
        jnp.bfloat16
    )
    conv_heads = conv_x.reshape(per_device_share, length_value, groups_dev, per_group, head_size)
    intra = jnp.einsum(
        "rghts,rsghp->rtghp", mix_weights, conv_heads, preferred_element_type=jnp.float32
    )
    inter = (
        jnp.einsum("rtgn,rghpn->rtghp", c_proj, cached_state, preferred_element_type=jnp.float32)
        * jnp.exp(log_decay5)[..., None]
    )
    skip_gain = head_skip_gain.reshape(groups_dev, per_group)[..., None]
    mixed = intra + inter + skip_gain * conv_heads
    mean_square = jnp.mean(mixed * mixed, axis=(3, 4), keepdims=True)
    normed_output = (
        (mixed * lax.rsqrt(mean_square + NORM_EPSILON)).reshape(
            per_device_share, length_value, hidden_features_on_card
        )
        * group_norm_gain
    ).astype(jnp.bfloat16)
    low_partial = jnp.einsum(
        "rtc,qc->rtq", normed_output, down_t, preferred_element_type=jnp.float32
    )
    reduced_rank = lax.psum(low_partial, "head").astype(jnp.bfloat16)
    adapter_output_term = (
        jnp.einsum("rtq,rqd->rtd", reduced_rank, up_panel, preferred_element_type=jnp.float32)
        * ADAPTER_SCALE
    ).astype(jnp.bfloat16)
    log_total = log_decay[:, -1:, :]
    carry_weight = (jnp.exp(log_total - log_decay) * step_size).reshape(
        per_device_share, length_value, groups_dev, per_group
    )
    carried = (conv_heads * carry_weight[..., None]).astype(jnp.bfloat16)
    fresh_state = jnp.einsum(
        "rsghp,rsgn->rghpn", carried, b_proj, preferred_element_type=jnp.float32
    )
    keep_factor = jnp.exp(log_total[:, 0]).reshape(per_device_share, groups_dev, per_group)[
        ..., None, None
    ]
    updated_state = fresh_state + keep_factor * cached_state
    return (
        normed_output.reshape(per_device_share * length_value, hidden_features_on_card),
        adapter_output_term.reshape(per_device_share * length_value, model_per_device),
        updated_state.reshape(per_device_share, heads_dev, head_size, state_size).astype(
            jnp.bfloat16
        ),
    )


def solution(mesh):
    return jax.shard_map(
        per_device,
        mesh=mesh,
        in_specs=(
            P("req", "head"),
            P("req", "head", None, None),
            P("req", "head"),
            P(None, "head"),
            P(None, "head", None, None),
            P("head"),
            P("head"),
            P("head"),
            P("head"),
            P("req"),
            P(),
            P("req"),
            P("req"),
            P("req", "head", None),
            P("req", None, "head"),
            P("req", "head", None, None),
            P("req", None, "head"),
            P("req", None, "head", None, None),
        ),
        out_specs=(P("req", "head"), P("req", "head"), P("req", "head", None, None)),
        check_vma=False,
    )
```

```python
import functools

import jax
import jax.numpy as jnp
from jax import lax
from jax.experimental import pallas as pl
from jax.experimental.pallas import tpu as pltpu
from jax.sharding import PartitionSpec as P

ADAPTER_SCALE = 2.0
NORM_EPSILON = 1e-05


def causal_conv(cached, current, weight):
    joined = jnp.concatenate([cached, current], axis=1)
    length_value = current.shape[1]
    summed = weight[0] * joined[:, 0:length_value]
    for tap in range(1, weight.shape[0]):
        summed = summed + weight[tap] * joined[:, tap : tap + length_value]
    return jax.nn.silu(summed).astype(jnp.bfloat16)


def exchange_kernel(
    n,
    numbers_ref,
    small_ref,
    meta_ref,
    conv_ref,
    meta_land,
    landed,
    picked,
    conv_land,
    table,
    meta_send,
    meta_recv,
    first_send,
    first_recv,
    second_send,
    second_recv,
    table_sem,
):
    me = lax.axis_index("req")

    def peer_of(step):
        return lax.rem(me + step, n)

    def remote(src, dst, send, recv, step):
        return pltpu.make_async_remote_copy(
            src_ref=src,
            dst_ref=dst,
            send_sem=send.at[step],
            recv_sem=recv.at[step],
            device_id={"req": peer_of(step)},
            device_id_type=pl.DeviceIdType.MESH,
        )

    def meta_copy(step):
        return remote(numbers_ref, meta_land.at[me], meta_send, meta_recv, step)

    def first_copy(step):
        return remote(small_ref.at[peer_of(step)], landed.at[me], first_send, first_recv, step)

    def second_copy(step):
        return remote(picked.at[peer_of(step)], conv_land.at[me], second_send, second_recv, step)

    barrier = pltpu.get_barrier_semaphore()

    def greet(step, carry):
        pl.semaphore_signal(
            barrier,
            inc=1,
            device_id={"req": peer_of(step)},
            device_id_type=pl.DeviceIdType.MESH,
        )
        return carry

    lax.fori_loop(1, n, greet, 0)
    pl.semaphore_wait(barrier, n - 1)

    def send_first(step, carry):
        meta_copy(step).start()
        first_copy(step).start()
        return carry

    lax.fori_loop(1, n, send_first, 0)
    meta_land[me] = numbers_ref[...]
    landed[me] = small_ref[me]

    def wait_first(step, carry):
        meta_copy(step).wait()
        first_copy(step).wait()
        return carry

    lax.fori_loop(1, n, wait_first, 0)
    to_table = pltpu.make_async_copy(meta_land, table, table_sem)
    to_table.start()
    to_table.wait()

    def pick(request):
        return landed[table[request, 0, 1], table[request, 0, 2]]

    def send_second(step, carry):
        peer = peer_of(step)
        picked[peer] = pick(peer)
        second_copy(step).start()
        return carry

    lax.fori_loop(1, n, send_second, 0)
    conv_land[me] = pick(me)

    def wait_second(step, carry):
        second_copy(step).wait()
        return carry

    lax.fori_loop(1, n, wait_second, 0)
    meta_ref[...] = meta_land[...]
    conv_ref[...] = conv_land[...]


def exchange(n, numbers, small):
    slots, rows = small.shape[1], small.shape[2]
    in_vmem = pl.BlockSpec(memory_space=pltpu.VMEM)
    return pl.pallas_call(
        functools.partial(exchange_kernel, n),
        out_shape=(
            jax.ShapeDtypeStruct((n, 8, 128), jnp.int32),
            jax.ShapeDtypeStruct((n, rows, 128), jnp.bfloat16),
        ),
        in_specs=[in_vmem, in_vmem],
        out_specs=(in_vmem, in_vmem),
        scratch_shapes=[
            pltpu.VMEM((n, 8, 128), jnp.int32),
            pltpu.VMEM((n, slots, rows, 128), jnp.bfloat16),
            pltpu.VMEM((n, rows, 128), jnp.bfloat16),
            pltpu.VMEM((n, rows, 128), jnp.bfloat16),
            pltpu.SMEM((n, 8, 128), jnp.int32),
        ]
        + [pltpu.SemaphoreType.DMA((n,))] * 6
        + [pltpu.SemaphoreType.DMA],
        compiler_params=pltpu.CompilerParams(collective_id=0, has_side_effects=True),
        cost_estimate=pl.CostEstimate(
            flops=0, bytes_accessed=30_000_000, transcendentals=0
        ),
    )(numbers, small)


def per_device(
    inner_input,
    projection_input,
    step_before_bias,
    inner_conv_taps,
    projection_conv_taps,
    step_bias,
    head_decay_rate,
    head_skip_gain,
    group_norm_gain,
    tenant,
    tenant_adapter_row,
    cache_holder_index,
    cache_slot_index,
    adapter_down_panels,
    adapter_up_panels,
    cached_ssm_states,
    inner_conv_cache,
    projection_conv_cache,
):
    per_device_share = tenant.shape[0]
    slots_dev = cached_ssm_states.shape[0]
    hidden_features_on_card = inner_input.shape[1]
    heads_dev = step_before_bias.shape[1]
    groups_dev = projection_input.shape[1]
    state_size = projection_input.shape[3]
    head_size = hidden_features_on_card // heads_dev
    per_group = heads_dev // groups_dev
    reduced_width = adapter_down_panels.shape[2]
    model_per_device = adapter_up_panels.shape[2]
    tap_count = inner_conv_taps.shape[0]
    length_value = inner_input.shape[0] // per_device_share
    n = lax.axis_size("req")
    me = lax.axis_index("req")
    x_size = (tap_count - 1) * hidden_features_on_card
    flat = jnp.concatenate(
        [inner_conv_cache.reshape(slots_dev, -1), projection_conv_cache.reshape(slots_dev, -1)],
        axis=1,
    )
    flat_size = flat.shape[1]
    tiles = -(-flat_size // (n * 2048))
    small = jnp.pad(flat, ((0, 0), (0, n * tiles * 2048 - flat_size)))
    small = jnp.transpose(small.reshape(slots_dev, n, tiles * 16, 128), (1, 0, 2, 3))
    numbers = jnp.concatenate([tenant, cache_holder_index, cache_slot_index])
    numbers = jnp.broadcast_to(jnp.pad(numbers, (0, 128 - numbers.shape[0])), (8, 128))
    panels = jnp.concatenate(
        [
            jnp.transpose(adapter_down_panels[0].reshape(n, -1, reduced_width), (0, 2, 1)),
            jnp.transpose(adapter_up_panels[0].reshape(reduced_width, n, -1), (1, 0, 2)),
        ],
        axis=2,
    )
    down_piece = hidden_features_on_card // n
    panels = lax.all_to_all(panels, "req", split_axis=0, concat_axis=0, tiled=True)
    meta, conv_pieces = exchange(n, numbers, small)
    tenant_all, owner_all, slot_all = meta[:, 0, 0], meta[:, 0, 1], meta[:, 0, 2]
    picked_row = jnp.take(tenant_adapter_row, tenant_all, axis=0, mode="clip")
    my_slot = jnp.sum(jnp.where(owner_all == me, slot_all, 0))
    my_state = lax.dynamic_index_in_dim(cached_ssm_states, my_slot, 0, keepdims=False)
    state_pieces = my_state.reshape(n, heads_dev * head_size // n, state_size)
    state_pieces = lax.all_to_all(state_pieces, "req", split_axis=0, concat_axis=0, tiled=True)
    state_pieces = jnp.take(state_pieces, owner_all, axis=0, mode="clip")
    state_pieces = lax.all_to_all(state_pieces, "req", split_axis=0, concat_axis=0, tiled=True)
    panels = jnp.take(panels, picked_row, axis=0, mode="clip")
    panels, state_pieces = lax.optimization_barrier((panels, state_pieces))
    panels = lax.all_to_all(panels, "req", split_axis=0, concat_axis=0, tiled=True)
    down_t = jnp.transpose(panels[:, :, :down_piece], (1, 0, 2)).reshape(
        reduced_width, hidden_features_on_card
    )
    up_panel = jnp.transpose(panels[:, :, down_piece:], (1, 0, 2)).reshape(
        per_device_share, reduced_width, model_per_device
    )
    cached_state = state_pieces.reshape(
        per_device_share, groups_dev, per_group, head_size, state_size
    )
    mine = conv_pieces.reshape(1, -1)
    cached_x = mine[:, :x_size].reshape(1, tap_count - 1, hidden_features_on_card)
    cached_bc = mine[:, x_size:flat_size].reshape(1, tap_count - 1, groups_dev, 2, state_size)
    conv_x = causal_conv(
        cached_x,
        inner_input.reshape(per_device_share, length_value, hidden_features_on_card),
        inner_conv_taps,
    )
    conv_bc = causal_conv(
        cached_bc,
        projection_input.reshape(per_device_share, length_value, groups_dev, 2, state_size),
        projection_conv_taps,
    )
    b_proj = conv_bc[:, :, :, 0]
    c_proj = conv_bc[:, :, :, 1]
    step_size = jax.nn.softplus(step_before_bias.astype(jnp.float32) + step_bias).reshape(
        per_device_share, length_value, heads_dev
    )
    log_decay = jnp.cumsum(-head_decay_rate * step_size, axis=1)
    log_decay5 = log_decay.reshape(per_device_share, length_value, groups_dev, per_group)
    step_size5 = step_size.reshape(per_device_share, length_value, groups_dev, per_group)
    score_bc = jnp.einsum("rtgn,rsgn->rgts", c_proj, b_proj, preferred_element_type=jnp.float32)
    decay_rows = jnp.transpose(log_decay5, (0, 2, 3, 1))
    log_gap = decay_rows[..., :, None] - decay_rows[..., None, :]
    token_ids = jnp.arange(length_value, dtype=jnp.int32)
    causal = token_ids[:, None] >= token_ids[None, :]
    decay_factor = jnp.exp(jnp.where(causal, log_gap, -jnp.inf))
    step_rows = jnp.transpose(step_size5, (0, 2, 3, 1))
    mix_weights = (score_bc[:, :, None] * decay_factor * step_rows[..., None, :]).astype(
        jnp.bfloat16
    )
    conv_heads = conv_x.reshape(per_device_share, length_value, groups_dev, per_group, head_size)
    intra = jnp.einsum(
        "rghts,rsghp->rtghp", mix_weights, conv_heads, preferred_element_type=jnp.float32
    )
    inter = (
        jnp.einsum("rtgn,rghpn->rtghp", c_proj, cached_state, preferred_element_type=jnp.float32)
        * jnp.exp(log_decay5)[..., None]
    )
    skip_gain = head_skip_gain.reshape(groups_dev, per_group)[..., None]
    mixed = intra + inter + skip_gain * conv_heads
    mean_square = jnp.mean(mixed * mixed, axis=(3, 4), keepdims=True)
    normed_output = (
        (mixed * lax.rsqrt(mean_square + NORM_EPSILON)).reshape(
            per_device_share, length_value, hidden_features_on_card
        )
        * group_norm_gain
    ).astype(jnp.bfloat16)
    low_partial = jnp.einsum(
        "rtc,qc->rtq", normed_output, down_t, preferred_element_type=jnp.float32
    )
    reduced_rank = lax.psum(low_partial, "head").astype(jnp.bfloat16)
    adapter_output_term = (
        jnp.einsum("rtq,rqd->rtd", reduced_rank, up_panel, preferred_element_type=jnp.float32)
        * ADAPTER_SCALE
    ).astype(jnp.bfloat16)
    log_total = log_decay[:, -1:, :]
    carry_weight = (jnp.exp(log_total - log_decay) * step_size).reshape(
        per_device_share, length_value, groups_dev, per_group
    )
    carried = (conv_heads * carry_weight[..., None]).astype(jnp.bfloat16)
    fresh_state = jnp.einsum(
        "rsghp,rsgn->rghpn", carried, b_proj, preferred_element_type=jnp.float32
    )
    keep_factor = jnp.exp(log_total[:, 0]).reshape(per_device_share, groups_dev, per_group)[
        ..., None, None
    ]
    updated_state = fresh_state + keep_factor * cached_state
    return (
        normed_output.reshape(per_device_share * length_value, hidden_features_on_card),
        adapter_output_term.reshape(per_device_share * length_value, model_per_device),
        updated_state.reshape(per_device_share, heads_dev, head_size, state_size).astype(
            jnp.bfloat16
        ),
    )


def solution(mesh):
    return jax.shard_map(
        per_device,
        mesh=mesh,
        in_specs=(
            P("req", "head"),
            P("req", "head", None, None),
            P("req", "head"),
            P(None, "head"),
            P(None, "head", None, None),
            P("head"),
            P("head"),
            P("head"),
            P("head"),
            P("req"),
            P(),
            P("req"),
            P("req"),
            P("req", "head", None),
            P("req", None, "head"),
            P("req", "head", None, None),
            P("req", None, "head"),
            P("req", None, "head", None, None),
        ),
        out_specs=(P("req", "head"), P("req", "head"), P("req", "head", None, None)),
        check_vma=False,
    )
```

```python
import functools

import jax
import jax.numpy as jnp
from jax import lax
from jax.experimental import pallas as pl
from jax.experimental.pallas import tpu as pltpu
from jax.sharding import PartitionSpec as P

ADAPTER_SCALE = 2.0
NORM_EPSILON = 1e-05


def causal_conv(cached, current, weight):
    joined = jnp.concatenate([cached, current], axis=1)
    length_value = current.shape[1]
    summed = weight[0] * joined[:, 0:length_value]
    for tap in range(1, weight.shape[0]):
        summed = summed + weight[tap] * joined[:, tap : tap + length_value]
    return jax.nn.silu(summed).astype(jnp.bfloat16)


def exchange_kernel(
    n,
    numbers_ref,
    small_ref,
    meta_ref,
    conv_ref,
    meta_land,
    landed,
    picked,
    conv_land,
    table,
    meta_send,
    meta_recv,
    first_send,
    first_recv,
    second_send,
    second_recv,
    table_sem,
):
    me = lax.axis_index("req")

    def peer_of(step):
        return lax.rem(me + step, n)

    def remote(src, dst, send, recv, step):
        return pltpu.make_async_remote_copy(
            src_ref=src,
            dst_ref=dst,
            send_sem=send.at[step],
            recv_sem=recv.at[step],
            device_id={"req": peer_of(step)},
            device_id_type=pl.DeviceIdType.MESH,
        )

    def meta_copy(step):
        return remote(numbers_ref, meta_land.at[me], meta_send, meta_recv, step)

    def first_copy(step):
        return remote(small_ref.at[peer_of(step)], landed.at[me], first_send, first_recv, step)

    def second_copy(step):
        return remote(picked.at[peer_of(step)], conv_land.at[me], second_send, second_recv, step)

    barrier = pltpu.get_barrier_semaphore()

    def greet(step, carry):
        pl.semaphore_signal(
            barrier,
            inc=1,
            device_id={"req": peer_of(step)},
            device_id_type=pl.DeviceIdType.MESH,
        )
        return carry

    lax.fori_loop(1, n, greet, 0)
    pl.semaphore_wait(barrier, n - 1)

    def send_first(step, carry):
        meta_copy(step).start()
        first_copy(step).start()
        return carry

    lax.fori_loop(1, n, send_first, 0)
    meta_land[me] = numbers_ref[...]
    landed[me] = small_ref[me]

    def wait_first(step, carry):
        meta_copy(step).wait()
        first_copy(step).wait()
        return carry

    lax.fori_loop(1, n, wait_first, 0)
    to_table = pltpu.make_async_copy(meta_land, table, table_sem)
    to_table.start()
    to_table.wait()

    def pick(request):
        return landed[table[request, 0, 1], table[request, 0, 2]]

    def send_second(step, carry):
        peer = peer_of(step)
        picked[peer] = pick(peer)
        second_copy(step).start()
        return carry

    lax.fori_loop(1, n, send_second, 0)
    conv_land[me] = pick(me)

    def wait_second(step, carry):
        second_copy(step).wait()
        return carry

    lax.fori_loop(1, n, wait_second, 0)
    meta_ref[...] = meta_land[...]
    conv_ref[...] = conv_land[...]


def exchange(n, numbers, small):
    slots, rows = small.shape[1], small.shape[2]
    in_vmem = pl.BlockSpec(memory_space=pltpu.VMEM)
    return pl.pallas_call(
        functools.partial(exchange_kernel, n),
        out_shape=(
            jax.ShapeDtypeStruct((n, 8, 128), jnp.int32),
            jax.ShapeDtypeStruct((n, rows, 128), jnp.bfloat16),
        ),
        in_specs=[in_vmem, in_vmem],
        out_specs=(in_vmem, in_vmem),
        scratch_shapes=[
            pltpu.VMEM((n, 8, 128), jnp.int32),
            pltpu.VMEM((n, slots, rows, 128), jnp.bfloat16),
            pltpu.VMEM((n, rows, 128), jnp.bfloat16),
            pltpu.VMEM((n, rows, 128), jnp.bfloat16),
            pltpu.SMEM((n, 8, 128), jnp.int32),
        ]
        + [pltpu.SemaphoreType.DMA((n,))] * 6
        + [pltpu.SemaphoreType.DMA],
        compiler_params=pltpu.CompilerParams(collective_id=0, has_side_effects=True),
        cost_estimate=pl.CostEstimate(
            flops=0, bytes_accessed=30_000_000, transcendentals=0
        ),
    )(numbers, small)


def per_device(
    inner_input,
    projection_input,
    step_before_bias,
    inner_conv_taps,
    projection_conv_taps,
    step_bias,
    head_decay_rate,
    head_skip_gain,
    group_norm_gain,
    tenant,
    tenant_adapter_row,
    cache_holder_index,
    cache_slot_index,
    adapter_down_panels,
    adapter_up_panels,
    cached_ssm_states,
    inner_conv_cache,
    projection_conv_cache,
):
    per_device_share = tenant.shape[0]
    slots_dev = cached_ssm_states.shape[0]
    hidden_features_on_card = inner_input.shape[1]
    heads_dev = step_before_bias.shape[1]
    groups_dev = projection_input.shape[1]
    state_size = projection_input.shape[3]
    head_size = hidden_features_on_card // heads_dev
    per_group = heads_dev // groups_dev
    reduced_width = adapter_down_panels.shape[2]
    model_per_device = adapter_up_panels.shape[2]
    tap_count = inner_conv_taps.shape[0]
    length_value = inner_input.shape[0] // per_device_share
    n = lax.axis_size("req")
    me = lax.axis_index("req")
    x_size = (tap_count - 1) * hidden_features_on_card
    flat = jnp.concatenate(
        [inner_conv_cache.reshape(slots_dev, -1), projection_conv_cache.reshape(slots_dev, -1)],
        axis=1,
    )
    flat_size = flat.shape[1]
    tiles = -(-flat_size // (n * 2048))
    small = jnp.pad(flat, ((0, 0), (0, n * tiles * 2048 - flat_size)))
    small = jnp.transpose(small.reshape(slots_dev, n, tiles * 16, 128), (1, 0, 2, 3))
    numbers = jnp.concatenate([tenant, cache_holder_index, cache_slot_index])
    numbers = jnp.broadcast_to(jnp.pad(numbers, (0, 128 - numbers.shape[0])), (8, 128))
    panels = jnp.concatenate(
        [
            jnp.transpose(adapter_down_panels[0].reshape(n, -1, reduced_width), (0, 2, 1)),
            jnp.transpose(adapter_up_panels[0].reshape(reduced_width, n, -1), (1, 0, 2)),
        ],
        axis=2,
    )
    down_piece = hidden_features_on_card // n
    panels = lax.all_to_all(panels, "req", split_axis=0, concat_axis=0, tiled=True)
    meta, conv_pieces = exchange(n, numbers, small)
    tenant_all, owner_all, slot_all = meta[:, 0, 0], meta[:, 0, 1], meta[:, 0, 2]
    picked_row = jnp.take(tenant_adapter_row, tenant_all, axis=0, mode="clip")
    my_slot = jnp.sum(jnp.where(owner_all == me, slot_all, 0))
    my_state = lax.dynamic_index_in_dim(cached_ssm_states, my_slot, 0, keepdims=False)
    state_pieces = my_state.reshape(n, heads_dev * head_size // n, state_size)
    state_pieces, panels = lax.optimization_barrier((state_pieces, panels))
    state_pieces = lax.all_to_all(state_pieces, "req", split_axis=0, concat_axis=0, tiled=True)
    state_pieces = jnp.take(state_pieces, owner_all, axis=0, mode="clip")
    state_pieces = lax.all_to_all(state_pieces, "req", split_axis=0, concat_axis=0, tiled=True)
    panels = jnp.take(panels, picked_row, axis=0, mode="clip")
    panels, state_pieces = lax.optimization_barrier((panels, state_pieces))
    panels = lax.all_to_all(panels, "req", split_axis=0, concat_axis=0, tiled=True)
    down_t = jnp.transpose(panels[:, :, :down_piece], (1, 0, 2)).reshape(
        reduced_width, hidden_features_on_card
    )
    up_panel = jnp.transpose(panels[:, :, down_piece:], (1, 0, 2)).reshape(
        per_device_share, reduced_width, model_per_device
    )
    cached_state = state_pieces.reshape(
        per_device_share, groups_dev, per_group, head_size, state_size
    )
    mine = conv_pieces.reshape(1, -1)
    cached_x = mine[:, :x_size].reshape(1, tap_count - 1, hidden_features_on_card)
    cached_bc = mine[:, x_size:flat_size].reshape(1, tap_count - 1, groups_dev, 2, state_size)
    conv_x = causal_conv(
        cached_x,
        inner_input.reshape(per_device_share, length_value, hidden_features_on_card),
        inner_conv_taps,
    )
    conv_bc = causal_conv(
        cached_bc,
        projection_input.reshape(per_device_share, length_value, groups_dev, 2, state_size),
        projection_conv_taps,
    )
    b_proj = conv_bc[:, :, :, 0]
    c_proj = conv_bc[:, :, :, 1]
    step_size = jax.nn.softplus(step_before_bias.astype(jnp.float32) + step_bias).reshape(
        per_device_share, length_value, heads_dev
    )
    log_decay = jnp.cumsum(-head_decay_rate * step_size, axis=1)
    log_decay5 = log_decay.reshape(per_device_share, length_value, groups_dev, per_group)
    step_size5 = step_size.reshape(per_device_share, length_value, groups_dev, per_group)
    score_bc = jnp.einsum("rtgn,rsgn->rgts", c_proj, b_proj, preferred_element_type=jnp.float32)
    decay_rows = jnp.transpose(log_decay5, (0, 2, 3, 1))
    log_gap = decay_rows[..., :, None] - decay_rows[..., None, :]
    token_ids = jnp.arange(length_value, dtype=jnp.int32)
    causal = token_ids[:, None] >= token_ids[None, :]
    decay_factor = jnp.exp(jnp.where(causal, log_gap, -jnp.inf))
    step_rows = jnp.transpose(step_size5, (0, 2, 3, 1))
    mix_weights = (score_bc[:, :, None] * decay_factor * step_rows[..., None, :]).astype(
        jnp.bfloat16
    )
    conv_heads = conv_x.reshape(per_device_share, length_value, groups_dev, per_group, head_size)
    intra = jnp.einsum(
        "rghts,rsghp->rtghp", mix_weights, conv_heads, preferred_element_type=jnp.float32
    )
    inter = (
        jnp.einsum("rtgn,rghpn->rtghp", c_proj, cached_state, preferred_element_type=jnp.float32)
        * jnp.exp(log_decay5)[..., None]
    )
    skip_gain = head_skip_gain.reshape(groups_dev, per_group)[..., None]
    mixed = intra + inter + skip_gain * conv_heads
    mean_square = jnp.mean(mixed * mixed, axis=(3, 4), keepdims=True)
    normed_output = (
        (mixed * lax.rsqrt(mean_square + NORM_EPSILON)).reshape(
            per_device_share, length_value, hidden_features_on_card
        )
        * group_norm_gain
    ).astype(jnp.bfloat16)
    low_partial = jnp.einsum(
        "rtc,qc->rtq", normed_output, down_t, preferred_element_type=jnp.float32
    )
    reduced_rank = lax.psum(low_partial, "head").astype(jnp.bfloat16)
    adapter_output_term = (
        jnp.einsum("rtq,rqd->rtd", reduced_rank, up_panel, preferred_element_type=jnp.float32)
        * ADAPTER_SCALE
    ).astype(jnp.bfloat16)
    log_total = log_decay[:, -1:, :]
    carry_weight = (jnp.exp(log_total - log_decay) * step_size).reshape(
        per_device_share, length_value, groups_dev, per_group
    )
    carried = (conv_heads * carry_weight[..., None]).astype(jnp.bfloat16)
    fresh_state = jnp.einsum(
        "rsghp,rsgn->rghpn", carried, b_proj, preferred_element_type=jnp.float32
    )
    keep_factor = jnp.exp(log_total[:, 0]).reshape(per_device_share, groups_dev, per_group)[
        ..., None, None
    ]
    updated_state = fresh_state + keep_factor * cached_state
    return (
        normed_output.reshape(per_device_share * length_value, hidden_features_on_card),
        adapter_output_term.reshape(per_device_share * length_value, model_per_device),
        updated_state.reshape(per_device_share, heads_dev, head_size, state_size).astype(
            jnp.bfloat16
        ),
    )


def solution(mesh):
    return jax.shard_map(
        per_device,
        mesh=mesh,
        in_specs=(
            P("req", "head"),
            P("req", "head", None, None),
            P("req", "head"),
            P(None, "head"),
            P(None, "head", None, None),
            P("head"),
            P("head"),
            P("head"),
            P("head"),
            P("req"),
            P(),
            P("req"),
            P("req"),
            P("req", "head", None),
            P("req", None, "head"),
            P("req", "head", None, None),
            P("req", None, "head"),
            P("req", None, "head", None, None),
        ),
        out_specs=(P("req", "head"), P("req", "head"), P("req", "head", None, None)),
        check_vma=False,
    )
```
